32 devices in a mesh: shoot: 4 (over y, x), gx: 8 (over z, core).
Axes of the slice: x: 2, y: 2, z: 4, core: 2. Of those that a mesh axis runs over, the one named last changes fastest.
Arguments:
- start_states: float32 [4, 256, 64, 128], P('shoot', 'gx'), may hold values from 0.35 to 0.85
- initial_state: float32 [256, 64, 128], P('gx'), may hold values from 0.35 to 0.85
- x_velocity: float32 [256, 64, 128], P('gx'), may hold values from -1 to 1
- y_velocity: float32 [256, 64, 128], P('gx'), may hold values from -0.2 to 0.2
- z_velocity: float32 [256, 64, 128], P('gx'), may hold values from -0.2 to 0.2
- step_scale: float32 [256, 64, 128], P('gx'), may hold values from 0.13 to 0.26
- well_cells: int32 [8, 16], P('gx'), may hold values from 65536 to 196607, as said below
- well_rates: float32 [8, 16], P('gx'), may hold values from -0.8 to 0.8
- roster: int32 [4, 8, 16], P('shoot', 'gx'), may hold values 0 or 1
Outputs:
- end_states: float32 [4, 256, 64, 128], P('shoot', 'gx')
- defects: float32 [4, 256, 64, 128], P('shoot', 'gx')
The draws below stay inside these ranges and needn't reach their ends.
Inputs may be any that keep to these rules, and one draw needn't show every extreme that they name: `well_cells`: each entry is a flattened cell (x * 64 + z) * 128 + y of its own slab whose x lies from 8 to 23; cells may repeat.
All inputs are finite; a program needn't handle non-finite values. No bound on the sum of `roster` on one device may be relied on, other than what follows from the above.
Results may differ from the reference program's by a relative error of at most 0.00002.
Values sent between devices are 32-bit elements; how exact they have to be, the bound alone decides.
A program may use at most 128 MiB of HBM per device.

```python
import math
import jax
import jax.numpy as jnp
from jax import lax

CX = 32
NZ = 64
NY = 128
STEPS = 8
WELLS = 16
INTERVALS = 4
SLABS = 8
NX = 256


def draw_well_cells(key, part):
    key = jax.random.fold_in(key, 7)
    key_x, key_z, key_y = jax.random.split(key, 3)
    planes = jax.random.randint(key_x, (SLABS, WELLS), STEPS, CX - STEPS)
    depths = jax.random.randint(key_z, (SLABS, WELLS), 0, NZ)
    columns = jax.random.randint(key_y, (SLABS, WELLS), 0, NY)
    cells = (planes * NZ + depths) * NY + columns
    cells = cells.at[:, 0].set(STEPS * NZ * NY)
    cells = cells.at[:, 1].set((CX - STEPS) * NZ * NY - 1)
    return cells.astype(jnp.int32)


def draw_x_velocity(key, part):
    key = jax.random.fold_in(key, 11)
    key_sign, key_column, key_face = jax.random.split(key, 3)
    signs = (2 * jax.random.randint(key_sign, (NZ, NY), 0, 2) - 1).astype(jnp.float32)
    column = jax.random.uniform(key_column, (NZ, NY), jnp.float32, 0.85, 1.0)
    face = jax.random.uniform(key_face, (NX, NZ, NY), jnp.float32, 0.94, 1.0)
    return ((signs * column)[None] * face).astype(jnp.float32)


def set_ends(array, own_key, smallest, top_value):
    spot = [jax.random.randint(jax.random.fold_in(own_key, axis), (), 0, length) for axis, length in enumerate(array.shape)]
    main_axis = array.shape.index(max(array.shape))
    neighbour = spot[:main_axis] + [(spot[main_axis] + 1) % array.shape[main_axis]] + spot[main_axis + 1:]
    return array.at[tuple(spot)].set(smallest).at[tuple(neighbour)].set(top_value)


def level_of(stream_key, shape, shards, least, top_value):
    factor_of = 1.0
    for axis_at, parts in shards:
        draws = jax.random.uniform(jax.random.fold_in(jax.random.fold_in(stream_key, 6), axis_at), (parts,), jnp.float32, least / len(shards), top_value / len(shards))
        factor_of = factor_of * jnp.repeat(jnp.exp(draws), shape[axis_at] // parts).reshape((-1,) + (1,) * (len(shape) - 1 - axis_at))
    return factor_of


def setup_inputs(seed: int = 0) -> dict:
    arg_keys = jax.random.split(jax.random.key(seed), 10)
    start_states = jnp.clip(0.35 + 0.5 * jax.random.uniform(arg_keys[0], (INTERVALS, NX, NZ, NY), jnp.float32) ** level_of(arg_keys[0], (INTERVALS, NX, NZ, NY), ((0, 4), (1, 8)), -0.2, 0.2), 0.35, 0.85)
    initial_state = jnp.clip(0.35 + 0.5 * jax.random.uniform(arg_keys[1], (NX, NZ, NY), jnp.float32) ** level_of(arg_keys[1], (NX, NZ, NY), ((0, 8),), -0.2, 0.2), 0.35, 0.85)
    x_velocity = draw_x_velocity(jax.random.fold_in(arg_keys[9], 71), 0)
    y_velocity = jnp.clip(jax.random.uniform(arg_keys[3], (NX, NZ, NY), jnp.float32, -0.2, 0.2) * level_of(arg_keys[3], (NX, NZ, NY), ((0, 8),), -0.4, 0.0), -0.2, 0.2)
    z_velocity = jnp.clip(jax.random.uniform(arg_keys[4], (NX, NZ, NY), jnp.float32, -0.2, 0.2) * level_of(arg_keys[4], (NX, NZ, NY), ((0, 8),), -0.4, 0.0), -0.2, 0.2)
    step_scale = jnp.clip(jnp.exp(math.log(0.26) - 0.6931472 * jax.random.uniform(arg_keys[5], (NX, NZ, NY), jnp.float32) ** level_of(arg_keys[5], (NX, NZ, NY), ((0, 8),), -0.2, 0.2)), 0.13, 0.26)
    well_cells = draw_well_cells(jax.random.fold_in(arg_keys[9], 71), 0)
    well_rates = jnp.clip(jax.random.uniform(arg_keys[7], (SLABS, WELLS), jnp.float32, -0.8, 0.8) * level_of(arg_keys[7], (SLABS, WELLS), ((0, 8),), -0.4, 0.0), -0.8, 0.8)
    roster = set_ends((jax.random.randint(arg_keys[8], (INTERVALS, SLABS, WELLS), 0, 4) < 3).astype(jnp.int32), jax.random.fold_in(arg_keys[8], 1), 0, 1)
    return {"start_states": start_states, "initial_state": initial_state, "x_velocity": x_velocity, "y_velocity": y_velocity, "z_velocity": z_velocity, "step_scale": step_scale, "well_cells": well_cells, "well_rates": well_rates, "roster": roster}


def fraction(values):
    square = values * values
    return square / (square + 2.0 * (1.0 - values) ** 2)


def following(values, along):
    count = values.shape[along]
    inner = lax.slice_in_dim(values, 1, count, axis=along)
    zeros = jnp.zeros_like(lax.slice_in_dim(values, 0, 1, axis=along))
    return jnp.concatenate([inner, zeros], axis=along)


def preceding(values, along):
    count = values.shape[along]
    inner = lax.slice_in_dim(values, 0, count - 1, axis=along)
    zeros = jnp.zeros_like(lax.slice_in_dim(values, 0, 1, axis=along))
    return jnp.concatenate([zeros, inner], axis=along)


def face_flux(velocity, here, there):
    return jnp.maximum(velocity, 0.0) * here + jnp.minimum(velocity, 0.0) * there


def last_face_closed(velocity, along, offset, total):
    positions = offset + lax.broadcasted_iota(jnp.int32, velocity.shape, along)
    return jnp.where(positions < total - 1, velocity, jnp.zeros_like(velocity))


def net_flux(flow, x_closed, y_closed, z_closed):
    x_face = face_flux(x_closed, flow, following(flow, 0))
    z_face = face_flux(z_closed, flow, following(flow, 1))
    y_face = face_flux(y_closed, flow, following(flow, 2))
    return (x_face - preceding(x_face, 0)) + (z_face - preceding(z_face, 1)) + (y_face - preceding(y_face, 2))


def well_sources(flow_flat, cells, opened):
    terms = jnp.maximum(opened, 0.0) + jnp.minimum(opened, 0.0) * flow_flat[cells]
    return jnp.zeros_like(flow_flat).at[cells].add(terms)


def reference(start_states, initial_state, x_velocity, y_velocity, z_velocity, step_scale, well_cells, well_rates, roster):
    x_closed = last_face_closed(x_velocity, 0, 0, NX)
    z_closed = last_face_closed(z_velocity, 1, 0, NZ)
    y_closed = last_face_closed(y_velocity, 2, 0, NY)
    slab_offset = (jnp.arange(SLABS, dtype=jnp.int32) * (CX * NZ * NY)).astype(jnp.int32)
    cells = (well_cells + slab_offset[:, None]).astype(jnp.int32).reshape(-1)

    def run_interval(inputs):
        saturation, plan = inputs
        opened = (well_rates * plan.astype(well_rates.dtype)).reshape(-1)
        for turn in range(STEPS):
            flow = fraction(saturation)
            outflow = net_flux(flow, x_closed, y_closed, z_closed)
            sources = well_sources(flow.reshape(-1), cells, opened).reshape(flow.shape)
            saturation = saturation + step_scale * (sources - outflow)
        return saturation

    end_states = lax.map(run_interval, (start_states, roster))
    previous = jnp.concatenate([initial_state[None], end_states[:-1]], axis=0)
    defects = start_states - previous
    return end_states, defects
```

```python
import functools

import jax
import jax.numpy as jnp
from jax import lax
from jax.experimental import pallas as pl
from jax.experimental.pallas import tpu as pltpu
from jax.sharding import PartitionSpec as P

STEPS = 8
MESH = pl.DeviceIdType.MESH
PAD = 8


def tripled_fraction(s):
    square = s * s
    below = square + (2.0 / 3.0 - (4.0 / 3.0) * s)
    guess = pl.reciprocal(below, approx=True)
    return (square * guess) * (2.0 - below * guess)


def kernel(
    nx, nz, ny,
    start_hbm, initial_hbm, ux_hbm, uy_hbm, uz_hbm, scale_hbm, cells_ref, rates_ref, roster_ref,
    ends_hbm, defects_hbm,
    start, ux, uy, uz, scale, s_odd, s_even, f_even, f_odd, coef, add_well, mul_well, received, raw,
    load_sem, out_sem, first_send, first_recv, halo_send, halo_recv, end_send, end_recv,
):
    k, g = lax.axis_index("shoot"), lax.axis_index("gx")
    intervals, slabs = lax.axis_size("shoot"), lax.axis_size("gx")
    has_left, has_right = g > 0, g < slabs - 1
    has_before, has_after = k > 0, k < intervals - 1
    left, right, after, before = (k, g - 1), (k, g + 1), (k + 1, g), (k - 1, g)
    last = nx - 1
    rows = nx * nz
    base = PAD + nz
    half = nx // 2

    def plane(p, offset=0, count=1):
        first = p * nz if isinstance(p, int) else pl.multiple_of(p * nz, nz)
        return pl.ds(first + offset, count * nz)

    loads = [
        pltpu.make_async_copy(start_hbm, start, load_sem.at[0]),
        pltpu.make_async_copy(ux_hbm, ux.at[pl.ds(nz, rows)], load_sem.at[1]),
        pltpu.make_async_copy(uz_hbm, uz.at[pl.ds(PAD, rows)], load_sem.at[2]),
        pltpu.make_async_copy(uy_hbm, uy, load_sem.at[3]),
        pltpu.make_async_copy(scale_hbm, scale, load_sem.at[4]),
    ]
    for load in loads:
        load.start()
    initial_load = pltpu.make_async_copy(initial_hbm, received, load_sem.at[5])

    @pl.when(jnp.logical_not(has_before))
    def _():
        initial_load.start()

    blank = jnp.zeros((nz, ny), jnp.float32)
    for ref in (f_even, f_odd):
        ref[0:PAD, :] = blank[:PAD]
        ref[rows + 2 * nz + PAD :, :] = blank[:PAD]

        @pl.loop(0, nx + 2)
        def _(p):
            ref[plane(p, PAD), :] = blank

    ux[0:nz, :] = blank
    uz[0:PAD, :] = blank[:PAD]
    raw[0] = blank
    raw[1] = blank

    barrier = pltpu.get_barrier_semaphore()
    for there, target in ((has_left, left), (has_right, right), (has_before, before)):

        @pl.when(there)
        def _():
            pl.semaphore_signal(barrier, 1, device_id=target, device_id_type=MESH)

    peers = has_left.astype(jnp.int32) + has_right.astype(jnp.int32) + has_after.astype(jnp.int32)
    pl.semaphore_wait(barrier, peers)

    def remote(source, target, send, recv, device):
        return pltpu.make_async_remote_copy(
            src_ref=source, dst_ref=target, send_sem=send, recv_sem=recv,
            device_id=device, device_id_type=MESH,
        )

    first_left = remote(start_hbm.at[plane(0)], raw.at[1], first_send.at[0], first_recv.at[0], left)
    first_right = remote(start_hbm.at[plane(last)], raw.at[0], first_send.at[1], first_recv.at[1], right)
    face_right = remote(ux_hbm.at[plane(last)], ux.at[pl.ds(0, nz)], first_send.at[2], first_recv.at[2], right)

    @pl.when(has_left)
    def _():
        first_left.start()

    @pl.when(has_right)
    def _():
        first_right.start()
        face_right.start()

    well_rows = (nx - 2 * STEPS) * nz
    slots = cells_ref.shape[1]
    cells = cells_ref[...]
    opened = rates_ref[...] * roster_ref[...].astype(jnp.float32)
    row_of = lax.broadcasted_iota(jnp.int32, (well_rows, slots), 0) + STEPS * nz
    in_row = jnp.where(row_of == lax.shift_right_logical(cells, ny.bit_length() - 1), 1.0, 0.0)
    column_of = lax.broadcasted_iota(jnp.int32, (ny, slots), 0)
    in_column = column_of == jnp.bitwise_and(cells, ny - 1)
    for well, part in ((add_well, jnp.maximum(opened, 0.0)), (mul_well, jnp.minimum(opened, 0.0))):
        well[pl.ds(0, STEPS * nz), :] = jnp.zeros((STEPS * nz, ny), jnp.float32)
        well[pl.ds(rows - STEPS * nz, STEPS * nz), :] = jnp.zeros((STEPS * nz, ny), jnp.float32)
        well[pl.ds(STEPS * nz, well_rows), :] = lax.dot_general(
            in_row, jnp.where(in_column, part, 0.0), (((1,), (1,)), ((), ())),
            precision=lax.Precision.HIGHEST, preferred_element_type=jnp.float32,
        )

    for load in loads:
        load.wait()

    z_of = lax.broadcasted_iota(jnp.int32, (nz, ny), 0)
    y_of = lax.broadcasted_iota(jnp.int32, (nz, ny), 1)

    def prepare(p):
        here = plane(p)
        f_even[plane(p, base), :] = tripled_fraction(start[here, :])
        h = scale[here, :]
        third = h * (1.0 / 3.0)
        closed = jnp.logical_and(jnp.logical_not(has_right), p == last)
        u = jnp.where(closed, 0.0, ux[plane(p, nz), :])
        v = ux[plane(p), :]
        total = jnp.maximum(u, 0.0) - jnp.minimum(v, 0.0)
        coef[1, here, :] = -third * jnp.minimum(u, 0.0)
        coef[2, here, :] = third * jnp.maximum(v, 0.0)
        u = jnp.where(z_of == nz - 1, 0.0, uz[plane(p, PAD), :])
        v = jnp.where(z_of == 0, 0.0, uz[plane(p, PAD - 1), :])
        total = total + (jnp.maximum(u, 0.0) - jnp.minimum(v, 0.0))
        coef[3, here, :] = -third * jnp.minimum(u, 0.0)
        coef[4, here, :] = third * jnp.maximum(v, 0.0)
        u = jnp.where(y_of == ny - 1, 0.0, uy[here, :])
        v = jnp.where(y_of == 0, 0.0, pltpu.roll(uy[here, :], 1, 1))
        total = total + (jnp.maximum(u, 0.0) - jnp.minimum(v, 0.0))
        coef[5, here, :] = -third * jnp.minimum(u, 0.0)
        coef[6, here, :] = third * jnp.maximum(v, 0.0)
        coef[0, here, :] = third * (mul_well[here, :] - total)
        coef[7, here, :] = h * add_well[here, :]

    def advance(p, t):
        here = plane(p)
        s_old = start if t == 1 else (s_even if t % 2 else s_odd)
        s_new = s_odd if t % 2 else s_even
        f_old, f_new = (f_even, f_odd) if t % 2 else (f_odd, f_even)
        f = f_old[plane(p, base), :]
        x = coef[1, here, :] * f_old[plane(p, base + nz), :] + coef[2, here, :] * f_old[plane(p, base - nz), :]
        z = coef[3, here, :] * f_old[plane(p, base + 1), :] + coef[4, here, :] * f_old[plane(p, base - 1), :]
        y = coef[5, here, :] * pltpu.roll(f, ny - 1, 1) + coef[6, here, :] * pltpu.roll(f, 1, 1)
        s = (s_old[here, :] + coef[7, here, :]) + (coef[0, here, :] * f + (x + (z + y)))
        s_new[here, :] = s
        if t < STEPS:
            f_new[plane(p, base), :] = tripled_fraction(s)

    sent = []

    def deliver(p, count):
        i = len(sent)
        here = plane(p, 0, count)
        onward = remote(s_even.at[here], received.at[here], end_send.at[i], end_recv.at[i], after)
        store = pltpu.make_async_copy(s_even.at[here], ends_hbm.at[here], out_sem.at[0, i])
        back = pltpu.make_async_copy(received.at[here], defects_hbm.at[here], out_sem.at[1, i])
        sent.append((p, count, onward, store, back))

        @pl.when(has_after)
        def _():
            onward.start()

        store.start()

    margin = half - 4 - STEPS

    @pl.loop(margin, last - margin + 1)
    def _(p):
        prepare(p)

    for t in range(1, STEPS + 1):

        @pl.loop(0, half - margin - t)
        def _(i):
            advance(margin + t + 2 * i, t)
            advance(margin + t + 2 * i + 1, t)

    deliver(half - 4, 8)

    @pl.loop(1, margin)
    def _(p):
        prepare(p)
        prepare(last - p)

    @pl.when(has_left)
    def _():
        first_right.wait_recv()
        face_right.wait_recv()

    @pl.when(has_right)
    def _():
        first_left.wait_recv()

    prepare(0)
    prepare(last)
    f_even[pl.ds(PAD, nz), :] = tripled_fraction(raw[0])
    f_even[pl.ds(base + rows, nz), :] = tripled_fraction(raw[1])

    halos = {}

    def exchange(t):
        f = f_odd if t % 2 else f_even
        to_left = remote(
            f.at[plane(0, base)], f.at[pl.ds(base + rows, nz)], halo_send.at[0, t], halo_recv.at[0, t], left
        )
        to_right = remote(
            f.at[plane(last, base)], f.at[pl.ds(PAD, nz)], halo_send.at[1, t], halo_recv.at[1, t], right
        )
        halos[t] = (to_left, to_right)

        @pl.when(has_left)
        def _():
            to_left.start()

        @pl.when(has_right)
        def _():
            to_right.start()

    def halo_arrived(t):
        @pl.when(has_left)
        def _():
            halos[t][1].wait_recv()

        @pl.when(has_right)
        def _():
            halos[t][0].wait_recv()

    def halo_left(t):
        @pl.when(has_left)
        def _():
            halos[t][0].wait_send()

        @pl.when(has_right)
        def _():
            halos[t][1].wait_send()

    advance(0, 1)
    advance(last, 1)
    exchange(1)

    for t in range(1, STEPS + 1):

        @pl.loop(0, margin)
        def _(i):
            advance(t + i, t)
            advance(last - t - i, t)

    deliver(STEPS, margin)
    deliver(nx - STEPS - margin, margin)

    for e in range(1, STEPS + 1):
        if e > 1:
            halo_arrived(e - 1)
            if e > 2:
                halo_left(e - 2)
            advance(0, e)
            advance(last, e)
            if e < STEPS:
                exchange(e)
        for j in range(1, STEPS + 1 - e):
            advance(j, e + j)
            advance(last - j, e + j)
        deliver(STEPS - e, 1)
        deliver(nx - 1 - STEPS + e, 1)
    halo_left(STEPS - 1)

    @pl.when(jnp.logical_not(has_before))
    def _():
        initial_load.wait()

    for p, count, onward, store, back in sent:
        here = plane(p, 0, count)

        @pl.when(has_before)
        def _():
            onward.wait_recv()

        received[here, :] = start[here, :] - received[here, :]
        back.start()

    @pl.when(has_left)
    def _():
        first_left.wait_send()

    @pl.when(has_right)
    def _():
        first_right.wait_send()
        face_right.wait_send()

    for p, count, onward, store, back in sent:

        @pl.when(has_after)
        def _():
            onward.wait_send()

        store.wait()
        back.wait()


def local(start, initial, ux, uy, uz, scale, cells, rates, roster):
    nx, nz, ny = ux.shape
    rows = nx * nz
    flat = (rows, ny)
    chunks = 3 + 2 * STEPS
    f32 = jnp.float32
    wide = (rows + 2 * nz + 2 * PAD, ny)
    dma = pltpu.SemaphoreType.DMA
    in_vmem = pl.BlockSpec(memory_space=pltpu.VMEM)
    anywhere = pl.BlockSpec(memory_space=pl.ANY)
    ends, defects = pl.pallas_call(
        functools.partial(kernel, nx, nz, ny),
        out_shape=[jax.ShapeDtypeStruct(flat, f32)] * 2,
        in_specs=[anywhere] * 6 + [in_vmem] * 3,
        out_specs=[anywhere] * 2,
        scratch_shapes=[
            pltpu.VMEM(flat, f32),
            pltpu.VMEM((rows + nz, ny), f32),
            pltpu.VMEM(flat, f32),
            pltpu.VMEM((rows + PAD, ny), f32),
            pltpu.VMEM(flat, f32),
            pltpu.VMEM(flat, f32),
            pltpu.VMEM(flat, f32),
            pltpu.VMEM(wide, f32),
            pltpu.VMEM(wide, f32),
            pltpu.VMEM((8,) + flat, f32),
            pltpu.VMEM(flat, f32),
            pltpu.VMEM(flat, f32),
            pltpu.VMEM(flat, f32),
            pltpu.VMEM((2, nz, ny), f32),
            dma((6,)),
            dma((2, chunks)),
            dma((3,)),
            dma((3,)),
            dma((2, STEPS)),
            dma((2, STEPS)),
            dma((chunks,)),
            dma((chunks,)),
        ],
        compiler_params=pltpu.CompilerParams(
            collective_id=0, has_side_effects=True, vmem_limit_bytes=40 << 20
        ),
    )(
        start.reshape(flat), initial.reshape(flat), ux.reshape(flat), uy.reshape(flat),
        uz.reshape(flat), scale.reshape(flat), cells, rates, roster.reshape(1, -1),
    )
    return ends.reshape(start.shape), defects.reshape(start.shape)


def solution(mesh):
    x_split = P("gx", None, None)
    both = P("shoot", "gx", None, None)
    return jax.shard_map(
        local,
        mesh=mesh,
        in_specs=(both,) + (x_split,) * 5 + (P("gx", None), P("gx", None), P("shoot", "gx", None)),
        out_specs=(both, both),
        check_vma=False,
    )
```
